512 devices in a mesh: rep: 32 (over x_hi, y, core), fsdp: 16 (over z, x_lo).
Axes of the slice: x: 4 (x_hi: 2, x_lo: 2; x = x_hi * 2 + x_lo), y: 8, z: 8, core: 2. Of those that a mesh axis runs over, the one named last changes fastest.
Arguments:
- tokens: bfloat16 [98304, 4096], P(('rep', 'fsdp')), may hold values from -6 to 6
- norm_gain: float32 [32, 4096], P('rep'), may hold values from 0.25 to 1.75
- doc_ids: int32 [32, 3072], P('rep', 'fsdp'), may hold values from 0 to 7, never falling along the last dimension, each value on 1 to 768 neighbouring positions
- key_cotangent: bfloat16 [98304, 512], P(('rep', 'fsdp')), may hold values from -6 to 6
- numerator: float32 [32, 4096, 512], P('rep', 'fsdp'), may hold values from -6 to 6
- first_moment: float32 [32, 4096, 512], P('rep', 'fsdp'), may hold values from -4 to 4
- second_moment: float32 [32, 4096, 512], P('rep', 'fsdp'), may hold values from 0.05 to 2
- push_weight: float32 [32], P('rep'), may hold values from 0.5 to 2
- gossip_step: int32 [1], replicated, may hold values from 0 to 63
Outputs:
- keys: bfloat16 [98304, 512], P(('rep', 'fsdp'))
- numerator_new: float32 [32, 4096, 512], P('rep', 'fsdp')
- first_new: float32 [32, 4096, 512], P('rep', 'fsdp')
- second_new: float32 [32, 4096, 512], P('rep', 'fsdp')
- weight_new: float32 [32], P('rep')
The draws below stay inside these ranges and needn't reach their ends.
Inputs may be any that keep to these rules, and one draw needn't show every extreme that they name: `doc_ids`: within each replica's row the ids never fall; each of the 8 documents has 1 to 768 tokens, and one has exactly 768.
All inputs are finite; a program needn't handle non-finite values.
Results may differ from the reference program's by a relative error of at most 0.006.
Values may be sent and summed in bfloat16 or wider, within the bound.
No kernel may reach another device: no remote copies, remote signals or barrier semaphores. Data moves between devices by JAX's collectives and lax.ppermute only.
A program may use at most 64 MiB of HBM per device.

```python
import math
import jax
import jax.numpy as jnp
import numpy as np
from jax import lax

D = 4096
KVH = 4
HD = 128
DOCS = 8
TOK_DEV = 192
KW = 512
SEQ = 3072
TOKENS = 98304
N_REP = 32
N_FSDP = 16


def block_scale(rng, extent, shards, low, top_value):
    factor_of, own = 1.0, jax.random.fold_in(rng, 6)
    for position, shards_of in shards:
        heights = jnp.exp(jax.random.uniform(jax.random.fold_in(own, position), (shards_of,), jnp.float32, low / len(shards), top_value / len(shards)))
        factor_of = factor_of * jnp.repeat(heights, extent[position] // shards_of).reshape([-1 if axis == position else 1 for axis in range(len(extent))])
    return factor_of


def length_profile(number_of, total, reach, slope):
    weights = [(1 << 20) // math.isqrt(grade ** slope) + 1 for grade in range(2, number_of + 1)]
    spare, holding = total - reach - (number_of - 1), [1] * (number_of - 1)
    while spare > 0:
        free = [i for i in range(number_of - 1) if holding[i] < reach]
        pool, budget = sum([weights[i] for i in free]), spare
        for i in free:
            addition = min(reach - holding[i], max(1, budget * weights[i] // pool), spare)
            holding[i] = holding[i] + addition
            spare = spare - addition
    return np.array([reach] + holding)


def ragged(rng, amount, total, most, slope):
    if amount == 2:
        one = jax.random.randint(rng, (), max(1, total - most), min(most, total - 1) + 1)
        return jnp.stack([one, total - one])
    sizes = jnp.asarray(length_profile(amount, total, most, slope), jnp.int32)
    twos = (amount - 1) // 2
    giver, receiver = sizes[1:1 + 2 * twos:2], sizes[2:2 + 2 * twos:2]
    slack = jnp.minimum(giver - 1, most - receiver)
    passed = jax.random.randint(jax.random.fold_in(rng, 1), (twos,), 0, 1 << 20) % (slack + 1)
    sizes = sizes.at[1:1 + 2 * twos:2].set(giver - passed).at[2:2 + 2 * twos:2].set(receiver + passed)
    return sizes[jax.random.permutation(jax.random.fold_in(rng, 2), amount)]


def noise(stream_key, extent, deviation, limit, shards=(), held_as=jnp.bfloat16):
    values = jax.random.normal(stream_key, extent, jnp.float32) * deviation
    if len(shards) > 0:
        values = block_scale(stream_key, extent, shards, -0.22, 0.18) * values
    return jnp.clip(values, min=-limit, max=limit).astype(held_as)


def setup_inputs(seed: int = 0) -> dict:
    seeds = jax.random.split(jax.random.key(seed), 10)
    return {
        "tokens": noise(seeds[0], (TOKENS, D), 1.0, 6.0, ((0, 512),)),
        "norm_gain": jnp.clip(1.0 + 0.15 * jax.random.normal(seeds[1], (N_REP, D), jnp.float32), 0.25, 1.75),
        "doc_ids": jax.vmap(lambda own: jnp.searchsorted(jnp.cumsum(ragged(own, DOCS, SEQ, SEQ // 4, 0)), jnp.arange(SEQ), side="right"))(jax.random.split(seeds[2], N_REP)).reshape((N_REP, SEQ)).astype(jnp.int32),
        "key_cotangent": noise(seeds[3], (TOKENS, KW), 1.0, 6.0, ((0, 512),)),
        "numerator": noise(seeds[4], (N_REP, D, KW), 1.0, 6.0, ((0, 32), (1, 16)), jnp.float32),
        "first_moment": noise(seeds[5], (N_REP, D, KW), 0.5, 4.0, ((0, 32), (1, 16)), jnp.float32),
        "second_moment": jnp.clip(jnp.exp(math.log(2.0) - 3.6888794 * jax.random.uniform(seeds[6], (N_REP, D, KW), jnp.float32) ** block_scale(seeds[6], (N_REP, D, KW), ((0, 32), (1, 16)), -0.2, 0.2)), 0.05, 2.0),
        "push_weight": jnp.clip(jnp.exp(math.log(2.0) - 1.3862944 * jax.random.uniform(seeds[7], (N_REP,), jnp.float32) ** block_scale(seeds[7], (N_REP,), ((0, 32),), -0.2, 0.2)), 0.5, 2.0),
        "gossip_step": jax.random.randint(seeds[8], (1,), 0, 64).astype(jnp.int32),
    }


THETA = 1000000.0
BETA_ONE = 0.9
BETA_TWO = 0.95
STEP_RATE = 0.1
WEIGHT_DECAY = 0.2
EPSILON = 1e-08
NORM_EPSILON = 1e-05
FIRST_CORRECTION = 1.0 - 0.9 ** 10
SECOND_CORRECTION = 1.0 - 0.95 ** 10

def rotate_half(values):
    return jnp.concatenate([-values[..., HD // 2:], values[..., :HD // 2]], axis=-1)

def rotary_tables(positions):
    frequency = THETA ** (-(jnp.arange(HD // 2, dtype=jnp.float32) * 2.0 / HD))
    angles = positions.astype(jnp.float32)[:, None] * frequency[None, :]
    cosine = jnp.concatenate([jnp.cos(angles), jnp.cos(angles)], axis=-1)[:, None, :]
    sine = jnp.concatenate([jnp.sin(angles), jnp.sin(angles)], axis=-1)[:, None, :]
    return (cosine, sine)

def replica_step(item):
    tokens, norm_gain, doc_ids, key_cotangent, numerator, first_moment, second_moment, weight = item
    token_values = tokens.astype(jnp.float32)
    stats = lax.optimization_barrier(jnp.mean(token_values * token_values, axis=-1, keepdims=True))
    normed = (token_values * lax.rsqrt(stats + NORM_EPSILON) * norm_gain[None, :]).astype(jnp.bfloat16)
    model = (numerator / weight).astype(jnp.bfloat16)
    onehot = (doc_ids[:, None] == jnp.arange(DOCS, dtype=jnp.int32)[None, :]).astype(jnp.int32)
    counts = lax.optimization_barrier(jnp.sum(onehot, axis=0))
    starts = jnp.cumsum(counts) - counts
    positions = jnp.arange(SEQ, dtype=jnp.int32) - lax.optimization_barrier(jnp.sum(onehot * starts[None, :], axis=1))
    cosine, sine = rotary_tables(positions)
    pre = (jnp.dot(normed, model, preferred_element_type=jnp.float32) * D ** (-0.5)).reshape(SEQ, KVH, HD)
    keys = (pre * cosine + rotate_half(pre) * sine).reshape(SEQ, KW).astype(jnp.bfloat16)
    cotangent = key_cotangent.astype(jnp.float32).reshape(SEQ, KVH, HD)
    back = ((cotangent * cosine - rotate_half(cotangent * sine)) * D ** (-0.5)).reshape(SEQ, KW).astype(jnp.bfloat16)
    blocks = jnp.einsum('jtd,jtk->jdk', normed.reshape(N_FSDP, TOK_DEV, D).astype(jnp.float32), back.reshape(N_FSDP, TOK_DEV, KW).astype(jnp.float32), precision=lax.Precision.HIGHEST)
    rounded = lax.optimization_barrier(blocks.astype(jnp.bfloat16))
    grad = lax.optimization_barrier(jnp.sum(rounded.astype(jnp.float32), axis=0))
    first_new = BETA_ONE * first_moment + (1.0 - BETA_ONE) * grad
    second_new = BETA_TWO * second_moment + (1.0 - BETA_TWO) * grad * grad
    update = first_new / FIRST_CORRECTION / (jnp.sqrt(second_new / SECOND_CORRECTION) + EPSILON)
    half = numerator - STEP_RATE * (update + WEIGHT_DECAY * (numerator / weight))
    return (keys, half, first_new, second_new)

def reference(tokens, norm_gain, doc_ids, key_cotangent, numerator, first_moment, second_moment, push_weight, gossip_step):
    items = (tokens.reshape(N_REP, SEQ, D), norm_gain, doc_ids, key_cotangent.reshape(N_REP, SEQ, KW), numerator, first_moment, second_moment, push_weight)
    keys, half, first_new, second_new = lax.map(replica_step, items)
    bit_count = N_REP.bit_length() - 1
    exponent = (gossip_step[0] % bit_count).astype(jnp.int32)
    distance = jnp.left_shift(jnp.int32(1), exponent)
    source = ((jnp.arange(N_REP, dtype=jnp.int32) - distance) % N_REP).astype(jnp.int32)
    sent = 0.5 * half
    sent_weight = 0.5 * push_weight
    numerator_new = sent + sent[source]
    weight_new = sent_weight + sent_weight[source]
    return (keys.reshape(TOKENS, KW), numerator_new, first_new, second_new, weight_new)
```

```python
from functools import partial

import jax
import jax.numpy as jnp
from jax import lax
from jax.experimental import pallas as pl
from jax.experimental.pallas import tpu as pltpu
from jax.sharding import PartitionSpec as P

D = 4096
KVH = 4
HD = 128
DOCS = 8
KW = 512
TOK = 192
NZ = 8
ROWS = 256
HALF = NZ * ROWS


THETA = 1000000.0
BETA_ONE = 0.9
BETA_TWO = 0.95
STEP_RATE = 0.1
WEIGHT_DECAY = 0.2
EPSILON = 1e-08
NORM_EPSILON = 1e-05
FIRST_CORRECTION = 1.0 - 0.9**10
SECOND_CORRECTION = 1.0 - 0.95**10
SCALE = D ** (-0.5)

PARAMS = pltpu.CompilerParams(vmem_limit_bytes=32 * 1024 * 1024)
F32, BF16 = jnp.float32, jnp.bfloat16


def along_z(value, distance):
    route = [(f, ((f // 2 + distance) % NZ) * 2 + f % 2) for f in range(2 * NZ)]
    return lax.ppermute(value, "fsdp", route)


def swap_x(value):
    return lax.ppermute(value, "fsdp", [(f, f ^ 1) for f in range(2 * NZ)])


def norm_kernel(place, tokens, gain, cotangent, keep, send):
    z, x = place[0], place[1]
    send[:, HALF:] = cotangent[...]

    def rows_of(i, carry):
        rows = pl.ds(pl.multiple_of(i * 16, 16), 16)
        values = tokens[rows, :].astype(F32)
        scale = lax.rsqrt(jnp.mean(values * values, axis=-1, keepdims=True) + NORM_EPSILON)
        for o in range(NZ):
            for side, target in ((x, keep), (1 - x, send)):
                columns = pl.ds(pl.multiple_of((2 * lax.rem(z + o, NZ) + side) * ROWS, ROWS), ROWS)
                part = tokens[rows, columns].astype(F32) * scale * gain[:, columns]
                target[rows, o * ROWS : (o + 1) * ROWS] = part.astype(BF16)
        return carry

    lax.fori_loop(0, TOK // 16, rows_of, 0)


def normalise(place, tokens, gain, cotangent):
    return pl.pallas_call(
        norm_kernel,
        out_shape=(
            jax.ShapeDtypeStruct((TOK, HALF), BF16),
            jax.ShapeDtypeStruct((TOK, HALF + KW), BF16),
        ),
        in_specs=[pl.BlockSpec(memory_space=pltpu.SMEM)] + [pl.BlockSpec(memory_space=pltpu.VMEM)] * 3,
        out_specs=[pl.BlockSpec(memory_space=pltpu.VMEM)] * 2,
        compiler_params=PARAMS,
        cost_estimate=pl.CostEstimate(flops=8 * TOK * D, bytes_accessed=4 * TOK * D, transcendentals=0),
        name="normalise",
    )(place, tokens, gain, cotangent)


def rotate_rows(cotangent, cosine, sine):
    parts = []
    for h in range(KVH):
        y = cotangent[:, h * HD : (h + 1) * HD].astype(F32)
        s = y * sine
        turned = jnp.concatenate([-s[:, HD // 2 :], s[:, : HD // 2]], axis=-1)
        parts.append(((y * cosine - turned) * SCALE).astype(BF16))
    return jnp.concatenate(parts, axis=-1)


def grad_kernel(keep, recv, cotangent, cosine, sine, up_one, down_one, up_two, down_two, own, back):
    back[:TOK] = rotate_rows(cotangent[...], cosine[:TOK], sine[:TOK])
    back[TOK:] = rotate_rows(recv[:, HALF:], cosine[TOK:], sine[TOK:])
    over = (((0,), (0,)), ((), ()))

    def block(o):
        columns = slice(o * ROWS, (o + 1) * ROWS)
        return lax.dot_general(keep[:, columns], back[:TOK], over, preferred_element_type=F32) + lax.dot_general(
            recv[:, columns], back[TOK:], over, preferred_element_type=F32
        )

    half = block(4).astype(BF16)
    up_two[...] = half[: ROWS // 2]
    down_two[...] = half[ROWS // 2 :]
    up_one[:ROWS] = block(3).astype(BF16)
    down_one[:ROWS] = block(5).astype(BF16)
    up_one[ROWS:] = block(1).astype(BF16)
    down_one[ROWS:] = block(7).astype(BF16)
    own[:ROWS] = block(0)
    own[ROWS : 2 * ROWS] = block(2)
    own[2 * ROWS :] = block(6)


def grad_parts(keep, recv, cotangent, cosine, sine):
    shape = jax.ShapeDtypeStruct
    return pl.pallas_call(
        grad_kernel,
        out_shape=(
            shape((2 * ROWS, KW), BF16),
            shape((2 * ROWS, KW), BF16),
            shape((ROWS // 2, KW), BF16),
            shape((ROWS // 2, KW), BF16),
            shape((3 * ROWS, KW), F32),
        ),
        in_specs=[pl.BlockSpec(memory_space=pltpu.VMEM)] * 5,
        out_specs=[pl.BlockSpec(memory_space=pltpu.VMEM)] * 5,
        scratch_shapes=[pltpu.VMEM((2 * TOK, KW), BF16)],
        compiler_params=PARAMS,
        cost_estimate=pl.CostEstimate(flops=4 * TOK * HALF * KW, bytes_accessed=6 << 20, transcendentals=0),
        name="grad_parts",
    )(keep, recv, cotangent, cosine, sine)


def keys_kernel(place, keep, recv, model, own, other):
    z = place[0]

    def half_of(values):
        total = jnp.zeros((TOK, KW), F32)
        for o in range(NZ):
            rows = pl.ds(pl.multiple_of(lax.rem(z + o, NZ) * ROWS, ROWS), ROWS)
            total = total + jnp.dot(
                values[:, o * ROWS : (o + 1) * ROWS], model[rows, :], preferred_element_type=F32
            )
        return total

    other[...] = half_of(recv).astype(BF16)
    own[...] = half_of(keep)


def keys_parts(place, keep, recv, model):
    return pl.pallas_call(
        keys_kernel,
        out_shape=(jax.ShapeDtypeStruct((TOK, KW), F32), jax.ShapeDtypeStruct((TOK, KW), BF16)),
        in_specs=[pl.BlockSpec(memory_space=pltpu.SMEM)] + [pl.BlockSpec(memory_space=pltpu.VMEM)] * 3,
        out_specs=[pl.BlockSpec(memory_space=pltpu.VMEM)] * 2,
        compiler_params=PARAMS,
        cost_estimate=pl.CostEstimate(flops=4 * TOK * HALF * KW, bytes_accessed=5 << 20, transcendentals=0),
        name="keys_parts",
    )(place, keep, recv, model)


def push_by(distance, values):
    n = lax.axis_size("rep")
    return lax.ppermute(values, "rep", [((i - distance) % n, i) for i in range(n)])


def local(
    tokens,
    norm_gain,
    doc_ids,
    key_cotangent,
    numerator,
    first_moment,
    second_moment,
    push_weight,
    gossip_step,
):
    f = lax.axis_index("fsdp")
    z, x = f // 2, f % 2
    place = jnp.stack([z, x]).astype(jnp.int32)
    weight = push_weight[0]

    other_ids = swap_x(doc_ids)
    keep, send = normalise(place, tokens, norm_gain, key_cotangent)
    recv = swap_x(send)

    model = (numerator[0] / weight).astype(BF16)
    zs = [[2 * i + side for i in range(NZ)] for side in range(2)]
    models = lax.all_gather(model, "fsdp", axis=0, axis_index_groups=zs, tiled=True)

    ids = jnp.concatenate([doc_ids[0], other_ids[0]])
    documents = jnp.arange(DOCS, dtype=jnp.int32)[None, :]
    counts = jnp.sum((ids[:, None] == documents).astype(jnp.int32), axis=0, keepdims=True)
    behind_one, behind_two = along_z(counts, 1), along_z(counts, 2)
    before = jnp.where(z >= 1, behind_one, 0) + jnp.where(z >= 2, behind_two, 0)
    row = jnp.arange(TOK, dtype=jnp.int32)
    index = jnp.concatenate([x * TOK + row, (1 - x) * TOK + row])
    shift = jnp.where(ids[:, None] == documents, before, 0) - jnp.where(ids[:, None] > documents, counts, 0)
    positions = index + jnp.sum(shift, axis=1)
    frequency = THETA ** (-(jnp.arange(HD // 2, dtype=jnp.float32) * 2.0 / HD))
    frequency = jnp.concatenate([frequency, frequency])
    angles = positions.astype(jnp.float32)[:, None] * frequency[None, :]
    cosine, sine = jnp.cos(angles), jnp.sin(angles)

    up_one, down_one, up_two, down_two, own = grad_parts(keep, recv, key_cotangent, cosine, sine)
    up_one, down_one = along_z(up_one, 1), along_z(down_one, -1)
    up_two, down_two = along_z(up_two, 2), along_z(down_two, -2)
    zero = jnp.zeros((ROWS // 2, KW), F32)
    up = own[ROWS : 2 * ROWS] + up_one[:ROWS] + jnp.concatenate([up_two.astype(F32), zero])
    down = own[2 * ROWS :] + down_one[:ROWS] + jnp.concatenate([zero, down_two.astype(F32)])
    up, down = along_z(up.astype(BF16), 2), along_z(down.astype(BF16), -2)
    near = own[:ROWS] + up_one[ROWS:] + down_one[ROWS:]

    own_keys, other_keys = keys_parts(place, keep, recv, models)
    pre = (own_keys + swap_x(other_keys).astype(F32)) * SCALE
    pre = pre.reshape(TOK, KVH, HD)
    turned = jnp.concatenate([-pre[..., HD // 2 :], pre[..., : HD // 2]], axis=-1)
    keys = pre * cosine[:TOK, None, :] + turned * sine[:TOK, None, :]
    keys = keys.reshape(TOK, KW).astype(BF16)

    grad = near + up.astype(F32) + down.astype(F32)
    shard = numerator[0]
    first_new = BETA_ONE * first_moment[0] + (1.0 - BETA_ONE) * grad
    second_new = BETA_TWO * second_moment[0] + (1.0 - BETA_TWO) * grad * grad
    update = first_new / FIRST_CORRECTION / (jnp.sqrt(second_new / SECOND_CORRECTION) + EPSILON)
    half = shard - STEP_RATE * (update + WEIGHT_DECAY * (shard / weight))
    sent = 0.5 * half
    sent_weight = 0.5 * push_weight
    message = jnp.concatenate([sent, jnp.broadcast_to(sent_weight[:, None], (16, KW))]).astype(BF16)
    bit_count = lax.axis_size("rep").bit_length() - 1
    branches = [partial(push_by, 1 << exponent) for exponent in range(bit_count)]
    received = lax.switch(gossip_step[0] % bit_count, branches, message)
    numerator_new = sent + received[:ROWS]
    weight_new = sent_weight + received[ROWS, :1]
    return (keys, numerator_new[None], first_new[None], second_new[None], weight_new)


def solution(mesh):
    in_specs = (
        P(("rep", "fsdp"), None),
        P("rep", None),
        P("rep", "fsdp"),
        P(("rep", "fsdp"), None),
        P("rep", "fsdp", None),
        P("rep", "fsdp", None),
        P("rep", "fsdp", None),
        P("rep"),
        P(),
    )
    out_specs = (
        P(("rep", "fsdp"), None),
        P("rep", "fsdp", None),
        P("rep", "fsdp", None),
        P("rep", "fsdp", None),
        P("rep"),
    )
    return jax.shard_map(local, mesh=mesh, in_specs=in_specs, out_specs=out_specs, check_vma=False)
```

```python
from functools import partial

import jax
import jax.numpy as jnp
from jax import lax
from jax.experimental import pallas as pl
from jax.experimental.pallas import tpu as pltpu
from jax.sharding import PartitionSpec as P

D = 4096
KVH = 4
HD = 128
DOCS = 8
KW = 512
TOK = 192
NZ = 8
ROWS = 256
STEP = 48
CHUNKS = TOK // STEP
HALF = NZ * ROWS
FIRST = (3, 1, 5, 7, 4)
REST = (2, 6, 0)


THETA = 1000000.0
BETA_ONE = 0.9
BETA_TWO = 0.95
STEP_RATE = 0.1
WEIGHT_DECAY = 0.2
EPSILON = 1e-08
NORM_EPSILON = 1e-05
FIRST_CORRECTION = 1.0 - 0.9**10
SECOND_CORRECTION = 1.0 - 0.95**10
SCALE = D ** (-0.5)

PARAMS = pltpu.CompilerParams(vmem_limit_bytes=32 * 1024 * 1024)
LARGE = pltpu.CompilerParams(vmem_limit_bytes=57 * 1024 * 1024)
F32, BF16 = jnp.float32, jnp.bfloat16


def along_z(value, distance):
    route = [(f, ((f // 2 + distance) % NZ) * 2 + f % 2) for f in range(2 * NZ)]
    return lax.ppermute(value, "fsdp", route)


def along_z_by_core(value, distance):
    route = []
    for r in range(lax.axis_size("rep")):
        way = distance if r % 2 == 0 else -distance
        for f in range(2 * NZ):
            route.append((r * 2 * NZ + f, r * 2 * NZ + ((f // 2 + way) % NZ) * 2 + f % 2))
    return lax.ppermute(value, ("rep", "fsdp"), route)


def swap_x(value):
    return lax.ppermute(value, "fsdp", [(f, f ^ 1) for f in range(2 * NZ)])


def whole(n):
    return [pl.BlockSpec(memory_space=pltpu.VMEM)] * n


def shapes(*pairs):
    return tuple(jax.ShapeDtypeStruct(shape, dtype) for shape, dtype in pairs)


def cost(size):
    return pl.CostEstimate(flops=0, bytes_accessed=size, transcendentals=0)


def place_of(z, o, side):
    return pl.ds(pl.multiple_of((2 * lax.rem(z + o, NZ) + side) * ROWS, ROWS), ROWS)


def scale_kernel(place, tokens, gain, cotangent, send_first, scales, held, gains, sems):
    z, x = place[0], place[1]
    copies = [pltpu.make_async_copy(gain, gains, sems.at[0])]
    for n in range(CHUNKS):
        rows = pl.ds(n * STEP, STEP)
        copies.append(pltpu.make_async_copy(tokens.at[rows], held.at[rows], sems.at[n + 1]))
    columns = pl.ds(len(FIRST) * ROWS, KW)
    copies.append(pltpu.make_async_copy(cotangent, send_first.at[:, columns], sems.at[CHUNKS + 1]))
    for copy in copies:
        copy.start()
    copies[0].wait()

    def rows_of(i, carry):
        rows = pl.ds(pl.multiple_of(i * 16, 16), 16)
        values = held[rows, :].astype(F32)
        scale = lax.rsqrt(jnp.mean(values * values, axis=-1, keepdims=True) + NORM_EPSILON)
        scales[rows, :] = jnp.broadcast_to(scale, (16, 128))
        for n, o in enumerate(FIRST):
            columns = place_of(z, o, 1 - x)
            part = held[rows, columns].astype(F32) * scale * gains[:, columns]
            send_first[rows, n * ROWS : (n + 1) * ROWS] = part.astype(BF16)
        return carry

    for n in range(CHUNKS):
        copies[n + 1].wait()
        lax.fori_loop(n * STEP // 16, (n + 1) * STEP // 16, rows_of, 0)
    copies[-1].wait()


def normalise_first(place, tokens, gain, cotangent):
    return pl.pallas_call(
        scale_kernel,
        out_shape=shapes(((TOK, len(FIRST) * ROWS + KW), BF16), ((TOK, 128), F32)),
        in_specs=[pl.BlockSpec(memory_space=pltpu.SMEM)] + [pl.BlockSpec(memory_space=pltpu.HBM)] * 3,
        out_specs=whole(2),
        scratch_shapes=[pltpu.VMEM((TOK, D), BF16), pltpu.VMEM((1, D), F32), pltpu.SemaphoreType.DMA((CHUNKS + 2,))],
        compiler_params=LARGE,
        cost_estimate=cost(1 << 10),
        name="normalise_first",
    )(place, tokens, gain, cotangent)


def norm_kernel(place, weight, tokens, gain, scales, numerator, keep, send_rest, model):
    z, x = place[0], place[1]
    model[...] = (numerator[0] / weight[0]).astype(BF16)

    def rows_of(i, carry):
        rows = pl.ds(pl.multiple_of(i * 16, 16), 16)
        scale = scales[rows, :1]

        def part(o, side):
            columns = place_of(z, o, side)
            return (tokens[rows, columns].astype(F32) * scale * gain[:, columns]).astype(BF16)

        for n, o in enumerate(FIRST + REST):
            keep[rows, n * ROWS : (n + 1) * ROWS] = part(o, x)
        for n, o in enumerate(REST):
            send_rest[rows, n * ROWS : (n + 1) * ROWS] = part(o, 1 - x)
        return carry

    lax.fori_loop(0, TOK // 16, rows_of, 0)


def normalise(place, weight, *operands):
    return pl.pallas_call(
        norm_kernel,
        out_shape=shapes(((TOK, HALF), BF16), ((TOK, len(REST) * ROWS), BF16), ((ROWS, KW), BF16)),
        in_specs=[pl.BlockSpec(memory_space=pltpu.SMEM)] * 2 + whole(4),
        out_specs=whole(3),
        compiler_params=PARAMS,
        cost_estimate=cost(1 << 10),
        name="normalise",
    )(place, weight, *operands)


def rotate_rows(cotangent, cosine, sine):
    parts = []
    for h in range(KVH):
        y = cotangent[:, h * HD : (h + 1) * HD].astype(F32)
        s = y * sine
        turned = jnp.concatenate([-s[:, HD // 2 :], s[:, : HD // 2]], axis=-1)
        parts.append(((y * cosine - turned) * SCALE).astype(BF16))
    return jnp.concatenate(parts, axis=-1)


OVER = (((0,), (0,)), ((), ()))


def grad_block(keep, recv, back, n):
    return lax.dot_general(
        keep[:, n * ROWS : (n + 1) * ROWS], back[:TOK], OVER, preferred_element_type=F32
    ) + lax.dot_general(recv[:, n * ROWS : (n + 1) * ROWS], back[TOK:], OVER, preferred_element_type=F32)


def first_kernel(keep, recv, cotangent, cosine, sine, three, one, five, seven, four, back):
    back[:TOK] = rotate_rows(cotangent[...], cosine[:TOK], sine[:TOK])
    back[TOK:] = rotate_rows(recv[:, len(FIRST) * ROWS :], cosine[TOK:], sine[TOK:])
    for n, target in enumerate((three, one, five, seven, four)):
        target[...] = grad_block(keep, recv, back, n).astype(BF16)


def first_parts(keep, recv, cotangent, cosine, sine):
    return pl.pallas_call(
        first_kernel,
        out_shape=shapes(*[((ROWS, KW), BF16)] * 5, ((2 * TOK, KW), BF16)),
        in_specs=whole(5),
        out_specs=whole(6),
        compiler_params=PARAMS,
        cost_estimate=cost(1 << 10),
        name="first_parts",
    )(keep, recv, cotangent, cosine, sine)


def rest_parts(keep, recv, back):
    columns = keep[:, len(FIRST) * ROWS :]
    return lax.dot_general(columns, back[:TOK], OVER, preferred_element_type=F32) + lax.dot_general(
        recv, back[TOK:], OVER, preferred_element_type=F32
    )


def turn_kernel(even, own, above, below, four, up, down):
    extra = four[...].astype(F32)
    share = jnp.full((ROWS, KW), even[0], F32) > 0.5
    up[...] = (own[:ROWS] + above[...].astype(F32) + jnp.where(share, extra, 0.0)).astype(BF16)
    down[...] = (own[ROWS : 2 * ROWS] + below[...].astype(F32) + jnp.where(share, 0.0, extra)).astype(BF16)


def turn(even, *operands):
    return pl.pallas_call(
        turn_kernel,
        out_shape=shapes(*[((ROWS, KW), BF16)] * 2),
        in_specs=[pl.BlockSpec(memory_space=pltpu.SMEM)] + whole(4),
        out_specs=whole(2),
        compiler_params=PARAMS,
        cost_estimate=cost(1 << 10),
        name="turn",
    )(even, *operands)


def near_kernel(even, keep, rest, zero, two, six, one, seven, above, below, far, own, other):
    for target, parts in ((above, (one, zero, six)), (below, (seven, zero, two))):
        for n, part in enumerate(parts):
            target[n * ROWS : (n + 1) * ROWS] = part[...]
    share = jnp.full((ROWS, KW), even[0], F32) > 0.5
    far[...] = jnp.where(share, six[...].astype(F32), two[...].astype(F32)).astype(BF16)
    total = jnp.zeros((TOK, KW), F32)
    for n, ref in enumerate((two, six, zero)):
        total += jnp.dot(rest[:, n * ROWS : (n + 1) * ROWS], ref[...], preferred_element_type=F32)
    other[...] = total
    total = jnp.zeros((TOK, KW), F32)
    for n, ref in enumerate((two, six, zero), len(FIRST)):
        total += jnp.dot(keep[:, n * ROWS : (n + 1) * ROWS], ref[...], preferred_element_type=F32)
    own[...] = total


def near_keys(even, *operands):
    return pl.pallas_call(
        near_kernel,
        out_shape=shapes(
            ((3 * ROWS, KW), BF16),
            ((3 * ROWS, KW), BF16),
            ((ROWS, KW), BF16),
            ((TOK, KW), F32),
            ((TOK, KW), F32),
        ),
        in_specs=[pl.BlockSpec(memory_space=pltpu.SMEM)] + whole(7),
        out_specs=whole(5),
        compiler_params=PARAMS,
        cost_estimate=cost(1 << 10),
        name="near_keys",
    )(even, *operands)


def keys_kernel(keep, first, below, above, far, near_own, near_other, own, other):
    model = {1: below[ROWS : 2 * ROWS], 3: below[2 * ROWS :], 7: above[ROWS : 2 * ROWS], 5: above[2 * ROWS :]}
    model[4] = far[...]
    total = near_other[...]
    for n, o in enumerate(FIRST):
        total += jnp.dot(first[:, n * ROWS : (n + 1) * ROWS], model[o], preferred_element_type=F32)
    other[...] = total.astype(BF16)
    total = near_own[...]
    for n, o in enumerate(FIRST):
        total += jnp.dot(keep[:, n * ROWS : (n + 1) * ROWS], model[o], preferred_element_type=F32)
    own[...] = total


def keys_parts(*operands):
    return pl.pallas_call(
        keys_kernel,
        out_shape=shapes(((TOK, KW), F32), ((TOK, KW), BF16)),
        in_specs=whole(7),
        out_specs=whole(2),
        compiler_params=PARAMS,
        cost_estimate=cost(1 << 10),
        name="keys_parts",
    )(*operands)


def finish_kernel(own, other, cosine, sine, keys):
    for h in range(KVH):
        columns = slice(h * HD, (h + 1) * HD)
        pre = (own[:, columns] + other[:, columns].astype(F32)) * SCALE
        turned = jnp.concatenate([-pre[:, HD // 2 :], pre[:, : HD // 2]], axis=-1)
        keys[:, columns] = (pre * cosine[:TOK] + turned * sine[:TOK]).astype(BF16)


def finish_keys(own, other, cosine, sine):
    return pl.pallas_call(
        finish_kernel,
        out_shape=jax.ShapeDtypeStruct((TOK, KW), BF16),
        in_specs=whole(4),
        out_specs=pl.BlockSpec(memory_space=pltpu.VMEM),
        compiler_params=PARAMS,
        cost_estimate=cost(1 << 10),
        name="finish_keys",
    )(own, other, cosine, sine)


def ready_kernel(weight, own, above, below, numerator, first, second, near, shard, moment, square):
    near[...] = own[2 * ROWS :] + above[:ROWS].astype(F32) + below[:ROWS].astype(F32)
    shard[...] = numerator[0] * (0.5 - 0.5 * STEP_RATE * WEIGHT_DECAY / weight[0])
    moment[...] = BETA_ONE * first[0]
    square[...] = BETA_TWO * second[0]


def ready(weight, *operands):
    return pl.pallas_call(
        ready_kernel,
        out_shape=shapes(*[((ROWS, KW), F32)] * 4),
        in_specs=[pl.BlockSpec(memory_space=pltpu.SMEM)] + whole(6),
        out_specs=whole(4),
        compiler_params=PARAMS,
        cost_estimate=cost(1 << 10),
        name="ready",
    )(weight, *operands)


def step(push_weight, near, shard, moment, square, up, down):
    grad = near + up.astype(F32) + down.astype(F32)
    first = moment + (1.0 - BETA_ONE) * grad
    second = square + (1.0 - BETA_TWO) * grad * grad
    root = jnp.sqrt(second * (1.0 / SECOND_CORRECTION)) + EPSILON
    half = shard - first * (0.5 * STEP_RATE / FIRST_CORRECTION) / root
    message = jnp.concatenate([half, jnp.broadcast_to(0.5 * push_weight[:, None], (16, KW))]).astype(BF16)
    return message, half, first[None], second[None]


def mix_kernel(weight, sent, received, numerator_new, weight_new):
    numerator_new[0] = sent[...] + received[:ROWS].astype(F32)
    weight_new[...] = 0.5 * weight[0] + received[ROWS : ROWS + 1, :128].astype(F32)


def mix(weight, sent, received):
    return pl.pallas_call(
        mix_kernel,
        out_shape=shapes(((1, ROWS, KW), F32), ((1, 128), F32)),
        in_specs=[pl.BlockSpec(memory_space=pltpu.SMEM)] + whole(2),
        out_specs=whole(2),
        compiler_params=PARAMS,
        cost_estimate=cost(1 << 10),
        name="mix",
    )(weight, sent, received)


def push_by(distance, message, keys_operands, cosine, sine):
    n = lax.axis_size("rep")
    received = lax.ppermute(message, "rep", [((i - distance) % n, i) for i in range(n)])
    own_keys, other_keys = keys_parts(*keys_operands)
    keys = finish_keys(own_keys, swap_x(other_keys), cosine, sine)
    return received, keys


def local(
    tokens,
    norm_gain,
    doc_ids,
    key_cotangent,
    numerator,
    first_moment,
    second_moment,
    push_weight,
    gossip_step,
):
    f = lax.axis_index("fsdp")
    z, x = f // 2, f % 2
    even = lax.axis_index("rep") % 2 == 0
    place = jnp.stack([z, x]).astype(jnp.int32)

    share = jnp.where(even, 1.0, 0.0).reshape(1).astype(F32)

    send_first, scales = normalise_first(place, tokens, norm_gain, key_cotangent)
    recv_first = swap_x(send_first)
    other_ids = swap_x(lax.optimization_barrier((doc_ids, scales))[0])
    pair_ids = jnp.concatenate([doc_ids[0], other_ids[0]])
    documents = jnp.arange(DOCS, dtype=jnp.int32)[None, :]
    counts = jnp.sum((pair_ids[:, None] == documents).astype(jnp.int32), axis=0, keepdims=True)
    scales, counts = lax.optimization_barrier((scales, counts))
    keep, send_rest, model = normalise(place, push_weight, tokens, norm_gain, scales, numerator)
    behind_one, behind_two = along_z(counts, 1), along_z(counts, 2)
    before = jnp.where(z >= 1, behind_one, 0) + jnp.where(z >= 2, behind_two, 0)
    row = jnp.arange(TOK, dtype=jnp.int32)
    index = jnp.concatenate([x * TOK + row, (1 - x) * TOK + row])
    shift = jnp.where(pair_ids[:, None] == documents, before, 0)
    shift = shift - jnp.where(pair_ids[:, None] > documents, counts, 0)
    positions = index + jnp.sum(shift, axis=1)
    frequency = THETA ** (-(jnp.arange(HD // 2, dtype=jnp.float32) * 2.0 / HD))
    frequency = jnp.concatenate([frequency, frequency])
    angles = positions.astype(jnp.float32)[:, None] * frequency[None, :]
    cosine, sine = jnp.cos(angles), jnp.sin(angles)

    three, one, five, seven, four, back = first_parts(keep, recv_first, key_cotangent, cosine, sine)
    three, five, four = along_z(three, 1), along_z(five, -1), along_z_by_core(four, 2)
    recv_rest = swap_x(send_rest)
    six, two = along_z(model, 2), along_z(model, -2)
    own = rest_parts(keep, recv_rest, back)
    above, below, far, near_own, near_other = near_keys(share, keep, recv_rest, model, two, six, one, seven)
    above, below, far = along_z(above, 1), along_z(below, -1), along_z_by_core(far, 2)

    up, down = turn(share, own, three, five, four)
    up, down = along_z(up, 2), along_z(down, -2)

    near = ready(push_weight, own, above, below, numerator, first_moment, second_moment)
    message, sent, first_new, second_new = step(push_weight, *near, up, down)
    bit_count = lax.axis_size("rep").bit_length() - 1
    branches = [partial(push_by, 1 << exponent) for exponent in range(bit_count)]
    operands = (keep, recv_first, below, above, far, near_own, near_other)
    received, keys = lax.switch(gossip_step[0] % bit_count, branches, message, operands, cosine, sine)
    numerator_new, weight_new = mix(push_weight, sent, received)
    return (keys, numerator_new, first_new, second_new, weight_new[0, :1])


def solution(mesh):
    in_specs = (
        P(("rep", "fsdp"), None),
        P("rep", None),
        P("rep", "fsdp"),
        P(("rep", "fsdp"), None),
        P("rep", "fsdp", None),
        P("rep", "fsdp", None),
        P("rep", "fsdp", None),
        P("rep"),
        P(),
    )
    out_specs = (
        P(("rep", "fsdp"), None),
        P("rep", "fsdp", None),
        P("rep", "fsdp", None),
        P("rep", "fsdp", None),
        P("rep"),
    )
    return jax.shard_map(local, mesh=mesh, in_specs=in_specs, out_specs=out_specs, check_vma=False)
```

```python
from functools import partial

import jax
import jax.numpy as jnp
from jax import lax
from jax.experimental import pallas as pl
from jax.experimental.pallas import tpu as pltpu
from jax.sharding import PartitionSpec as P

D = 4096
KVH = 4
HD = 128
DOCS = 8
KW = 512
TOK = 192
NZ = 8
ROWS = 256
STEP = 48
CHUNKS = TOK // STEP
HALF = NZ * ROWS
FIRST = (3, 1, 5, 7, 4)
REST = (2, 6, 0)


THETA = 1000000.0
BETA_ONE = 0.9
BETA_TWO = 0.95
STEP_RATE = 0.1
WEIGHT_DECAY = 0.2
EPSILON = 1e-08
NORM_EPSILON = 1e-05
FIRST_CORRECTION = 1.0 - 0.9**10
SECOND_CORRECTION = 1.0 - 0.95**10
SCALE = D ** (-0.5)

PARAMS = pltpu.CompilerParams(vmem_limit_bytes=32 * 1024 * 1024)
LARGE = pltpu.CompilerParams(vmem_limit_bytes=57 * 1024 * 1024)
F32, BF16 = jnp.float32, jnp.bfloat16


def along_z(value, distance):
    route = [(f, ((f // 2 + distance) % NZ) * 2 + f % 2) for f in range(2 * NZ)]
    return lax.ppermute(value, "fsdp", route)


def along_z_by_core(value, distance):
    route = []
    for r in range(lax.axis_size("rep")):
        way = distance if r % 2 == 0 else -distance
        for f in range(2 * NZ):
            route.append((r * 2 * NZ + f, r * 2 * NZ + ((f // 2 + way) % NZ) * 2 + f % 2))
    return lax.ppermute(value, ("rep", "fsdp"), route)


def swap_x(value):
    return lax.ppermute(value, "fsdp", [(f, f ^ 1) for f in range(2 * NZ)])


def whole(n):
    return [pl.BlockSpec(memory_space=pltpu.VMEM)] * n


def shapes(*pairs):
    return tuple(jax.ShapeDtypeStruct(shape, dtype) for shape, dtype in pairs)


def cost(size):
    return pl.CostEstimate(flops=0, bytes_accessed=size, transcendentals=0)


def place_of(z, o, side):
    return pl.ds(pl.multiple_of((2 * lax.rem(z + o, NZ) + side) * ROWS, ROWS), ROWS)


def place():
    f = lax.axis_index("fsdp")
    return lax.div(f, 2), lax.rem(f, 2)


def even_core():
    return lax.rem(lax.axis_index("rep"), 2) == 0


def scale_kernel(
    weight, tokens, gain, cotangent, numerator, send_first, scales, model, held, gains, shard, sems
):
    z, x = place()
    copies = [pltpu.make_async_copy(gain, gains, sems.at[0])]
    for n in range(CHUNKS):
        rows = pl.ds(n * STEP, STEP)
        copies.append(pltpu.make_async_copy(tokens.at[rows], held.at[rows], sems.at[n + 1]))
    columns = pl.ds(len(FIRST) * ROWS, KW)
    copies.append(pltpu.make_async_copy(cotangent, send_first.at[:, columns], sems.at[CHUNKS + 1]))
    copies.append(pltpu.make_async_copy(numerator.at[0], shard, sems.at[CHUNKS + 2]))
    for copy in copies:
        copy.start()
    copies[0].wait()

    def rows_of(i, carry):
        rows = pl.ds(pl.multiple_of(i * 16, 16), 16)
        values = held[rows, :].astype(F32)
        scale = lax.rsqrt(jnp.mean(values * values, axis=-1, keepdims=True) + NORM_EPSILON)
        scales[rows, :] = jnp.broadcast_to(scale, (16, 128))
        for n, o in enumerate(FIRST):
            columns = place_of(z, o, 1 - x)
            part = held[rows, columns].astype(F32) * scale * gains[:, columns]
            send_first[rows, n * ROWS : (n + 1) * ROWS] = part.astype(BF16)
        return carry

    for n in range(CHUNKS):
        copies[n + 1].wait()
        lax.fori_loop(n * STEP // 16, (n + 1) * STEP // 16, rows_of, 0)
    copies[-2].wait()
    copies[-1].wait()
    model[...] = (shard[...] / weight[0]).astype(BF16)


def normalise_first(weight, *operands):
    return pl.pallas_call(
        scale_kernel,
        out_shape=shapes(
            ((TOK, len(FIRST) * ROWS + KW), BF16),
            ((TOK, 128), F32),
            ((ROWS, KW), BF16),
        ),
        in_specs=[pl.BlockSpec(memory_space=pltpu.SMEM)] + [pl.BlockSpec(memory_space=pltpu.HBM)] * 4,
        out_specs=whole(3),
        scratch_shapes=[
            pltpu.VMEM((TOK, D), BF16),
            pltpu.VMEM((1, D), F32),
            pltpu.VMEM((ROWS, KW), F32),
            pltpu.SemaphoreType.DMA((CHUNKS + 3,)),
        ],
        compiler_params=LARGE,
        cost_estimate=cost(1 << 10),
        name="normalise_first",
    )(weight, *operands)


def norm_kernel(tokens, gain, scales, keep, send_rest):
    z, x = place()

    def rows_of(i, carry):
        rows = pl.ds(pl.multiple_of(i * 16, 16), 16)
        scale = scales[rows, :1]

        def part(o, side):
            columns = place_of(z, o, side)
            return (tokens[rows, columns].astype(F32) * scale * gain[:, columns]).astype(BF16)

        for n, o in enumerate(FIRST + REST):
            keep[rows, n * ROWS : (n + 1) * ROWS] = part(o, x)
        for n, o in enumerate(REST):
            send_rest[rows, n * ROWS : (n + 1) * ROWS] = part(o, 1 - x)
        return carry

    lax.fori_loop(0, TOK // 16, rows_of, 0)


def normalise(*operands):
    return pl.pallas_call(
        norm_kernel,
        out_shape=shapes(((TOK, HALF), BF16), ((TOK, len(REST) * ROWS), BF16)),
        in_specs=whole(3),
        out_specs=whole(2),
        compiler_params=PARAMS,
        cost_estimate=cost(1 << 10),
        name="normalise",
    )(*operands)


def rotate_rows(cotangent, cosine, sine):
    parts = []
    for h in range(KVH):
        y = cotangent[:, h * HD : (h + 1) * HD].astype(F32)
        s = y * sine
        turned = jnp.concatenate([-s[:, HD // 2 :], s[:, : HD // 2]], axis=-1)
        parts.append(((y * cosine - turned) * SCALE).astype(BF16))
    return jnp.concatenate(parts, axis=-1)


OVER = (((0,), (0,)), ((), ()))


def grad_block(keep, recv, back, n):
    return lax.dot_general(
        keep[:, n * ROWS : (n + 1) * ROWS], back[:TOK], OVER, preferred_element_type=F32
    ) + lax.dot_general(recv[:, n * ROWS : (n + 1) * ROWS], back[TOK:], OVER, preferred_element_type=F32)


def first_kernel(keep, recv, cotangent, cosine, sine, up, down, four, back):
    back[:TOK] = rotate_rows(cotangent[...], cosine[:TOK], sine[:TOK])
    back[TOK:] = rotate_rows(recv[:, len(FIRST) * ROWS :], cosine[TOK:], sine[TOK:])
    for n, target in enumerate((up.at[:ROWS], up.at[ROWS:], down.at[:ROWS], down.at[ROWS:], four)):
        target[...] = grad_block(keep, recv, back, n).astype(BF16)


def first_parts(keep, recv, cotangent, cosine, sine):
    return pl.pallas_call(
        first_kernel,
        out_shape=shapes(*[((2 * ROWS, KW), BF16)] * 2, ((ROWS, KW), BF16), ((2 * TOK, KW), BF16)),
        in_specs=whole(5),
        out_specs=whole(4),
        compiler_params=PARAMS,
        cost_estimate=cost(1 << 10),
        name="first_parts",
    )(keep, recv, cotangent, cosine, sine)


def rest_parts(keep, recv, back):
    columns = keep[:, len(FIRST) * ROWS :]
    return lax.dot_general(columns, back[:TOK], OVER, preferred_element_type=F32) + lax.dot_general(
        recv, back[TOK:], OVER, preferred_element_type=F32
    )


def turn_kernel(own, above, below, four, up, down):
    extra = four[...].astype(F32)
    share = jnp.full((ROWS, KW), even_core().astype(F32)) > 0.5
    up[...] = (own[:ROWS] + above[:ROWS].astype(F32) + jnp.where(share, extra, 0.0)).astype(BF16)
    down[...] = (own[ROWS : 2 * ROWS] + below[:ROWS].astype(F32) + jnp.where(share, 0.0, extra)).astype(BF16)


def turn(*operands):
    return pl.pallas_call(
        turn_kernel,
        out_shape=shapes(*[((ROWS, KW), BF16)] * 2),
        in_specs=whole(4),
        out_specs=whole(2),
        compiler_params=PARAMS,
        cost_estimate=cost(1 << 10),
        name="turn",
    )(*operands)


def second_kernel(zero, two, six, above, below, far):
    for target, parts in ((above, (zero, six)), (below, (zero, two))):
        for n, part in enumerate(parts):
            target[n * ROWS : (n + 1) * ROWS] = part[...]
    share = jnp.full((ROWS, KW), even_core().astype(F32)) > 0.5
    far[...] = jnp.where(share, six[...].astype(F32), two[...].astype(F32)).astype(BF16)


def second_rows(*operands):
    return pl.pallas_call(
        second_kernel,
        out_shape=shapes(*[((2 * ROWS, KW), BF16)] * 2, ((ROWS, KW), BF16)),
        in_specs=whole(3),
        out_specs=whole(3),
        compiler_params=PARAMS,
        cost_estimate=cost(1 << 10),
        name="second_rows",
    )(*operands)


def keys_kernel(keep, first, rest, zero, two, six, below, above, far, own, other):
    model = {0: zero[...], 2: two[...], 6: six[...], 4: far[...]}
    model.update({1: below[:ROWS], 3: below[ROWS:], 7: above[:ROWS], 5: above[ROWS:]})
    total = jnp.zeros((TOK, KW), F32)
    for blocks, ref in ((FIRST, first), (REST, rest)):
        for n, o in enumerate(blocks):
            total += jnp.dot(ref[:, n * ROWS : (n + 1) * ROWS], model[o], preferred_element_type=F32)
    other[...] = total.astype(BF16)
    total = jnp.zeros((TOK, KW), F32)
    for n, o in enumerate(FIRST + REST):
        total += jnp.dot(keep[:, n * ROWS : (n + 1) * ROWS], model[o], preferred_element_type=F32)
    own[...] = total


def keys_parts(*operands):
    return pl.pallas_call(
        keys_kernel,
        out_shape=shapes(((TOK, KW), F32), ((TOK, KW), BF16)),
        in_specs=whole(9),
        out_specs=whole(2),
        compiler_params=PARAMS,
        cost_estimate=cost(1 << 10),
        name="keys_parts",
    )(*operands)


def finish_kernel(own, other, cosine, sine, keys):
    for h in range(KVH):
        columns = slice(h * HD, (h + 1) * HD)
        pre = (own[:, columns] + other[:, columns].astype(F32)) * SCALE
        turned = jnp.concatenate([-pre[:, HD // 2 :], pre[:, : HD // 2]], axis=-1)
        keys[:, columns] = (pre * cosine[:TOK] + turned * sine[:TOK]).astype(BF16)


def finish_keys(own, other, cosine, sine):
    return pl.pallas_call(
        finish_kernel,
        out_shape=jax.ShapeDtypeStruct((TOK, KW), BF16),
        in_specs=whole(4),
        out_specs=pl.BlockSpec(memory_space=pltpu.VMEM),
        compiler_params=PARAMS,
        cost_estimate=cost(1 << 10),
        name="finish_keys",
    )(own, other, cosine, sine)


def ready_kernel(weight, own, above, below, numerator, first, second, near, shard, moment, square):
    near[...] = own[2 * ROWS :] + above[ROWS:].astype(F32) + below[ROWS:].astype(F32)
    shard[...] = numerator[0] * (0.5 - 0.5 * STEP_RATE * WEIGHT_DECAY / weight[0])
    moment[...] = BETA_ONE * first[0]
    square[...] = BETA_TWO * second[0]


def ready(weight, *operands):
    return pl.pallas_call(
        ready_kernel,
        out_shape=shapes(*[((ROWS, KW), F32)] * 4),
        in_specs=[pl.BlockSpec(memory_space=pltpu.SMEM)] + whole(6),
        out_specs=whole(4),
        compiler_params=PARAMS,
        cost_estimate=cost(1 << 10),
        name="ready",
    )(weight, *operands)


def step(push_weight, near, shard, moment, square, up, down):
    grad = near + up.astype(F32) + down.astype(F32)
    first = moment + (1.0 - BETA_ONE) * grad
    second = square + (1.0 - BETA_TWO) * grad * grad
    root = jnp.sqrt(second * (1.0 / SECOND_CORRECTION)) + EPSILON
    half = shard - first * (0.5 * STEP_RATE / FIRST_CORRECTION) / root
    message = jnp.concatenate([half, jnp.broadcast_to(0.5 * push_weight[:, None], (16, KW))]).astype(BF16)
    return message, half, first[None], second[None]


def mix_kernel(weight, sent, received, numerator_new, weight_new):
    numerator_new[0] = sent[...] + received[:ROWS].astype(F32)
    weight_new[...] = 0.5 * weight[0] + received[ROWS : ROWS + 1, :128].astype(F32)


def mix(weight, sent, received):
    return pl.pallas_call(
        mix_kernel,
        out_shape=shapes(((1, ROWS, KW), F32), ((1, 128), F32)),
        in_specs=[pl.BlockSpec(memory_space=pltpu.SMEM)] + whole(2),
        out_specs=whole(2),
        compiler_params=PARAMS,
        cost_estimate=cost(1 << 10),
        name="mix",
    )(weight, sent, received)


def push_by(distance, message):
    n = lax.axis_size("rep")
    return lax.ppermute(message, "rep", [((i - distance) % n, i) for i in range(n)])


def local(
    tokens,
    norm_gain,
    doc_ids,
    key_cotangent,
    numerator,
    first_moment,
    second_moment,
    push_weight,
    gossip_step,
):
    f = lax.axis_index("fsdp")
    x = f % 2


    send_first, scales, model = normalise_first(push_weight, tokens, norm_gain, key_cotangent, numerator)
    recv_first = swap_x(send_first)
    ids = jnp.broadcast_to(doc_ids[None], (2 * NZ, 1, TOK))
    ids = lax.all_to_all(ids, "fsdp", 0, 0, tiled=True)
    scales, ids, model = lax.optimization_barrier((scales, ids, model))
    keep, send_rest = normalise(tokens, norm_gain, scales)
    documents = jnp.arange(DOCS, dtype=jnp.int32)
    totals = jnp.sum((ids.reshape(1, -1) == documents[:, None]).astype(jnp.int32), axis=1)
    other = f + 1 - 2 * x
    pair_ids = jnp.concatenate([doc_ids[0], lax.dynamic_index_in_dim(ids, other, 0, False)[0]])
    row = jnp.arange(TOK, dtype=jnp.int32)
    index = jnp.concatenate([f * TOK + row, other * TOK + row])
    starts = jnp.sum(jnp.where(pair_ids[:, None] > documents[None, :], totals[None, :], 0), axis=1)
    positions = index - starts
    frequency = THETA ** (-(jnp.arange(HD // 2, dtype=jnp.float32) * 2.0 / HD))
    frequency = jnp.concatenate([frequency, frequency])
    angles = positions.astype(jnp.float32)[:, None] * frequency[None, :]
    cosine, sine = jnp.cos(angles), jnp.sin(angles)

    above, below, four, back = first_parts(keep, recv_first, key_cotangent, cosine, sine)
    above, below, four = along_z(above, 1), along_z(below, -1), along_z_by_core(four, 2)
    recv_rest = swap_x(send_rest)
    six, two = along_z(model, 2), along_z(model, -2)
    own = rest_parts(keep, recv_rest, back)
    model, six, two, own = lax.optimization_barrier((model, six, two, own))
    rows_above, rows_below, far = second_rows(model, two, six)
    rows_above, rows_below = along_z(rows_above, 1), along_z(rows_below, -1)
    far = along_z_by_core(far, 2)

    up, down = turn(own, above, below, four)
    up, down = along_z(up, 2), along_z(down, -2)

    own_keys, other_keys = keys_parts(
        keep, recv_first, recv_rest, model, two, six, rows_below, rows_above, far
    )
    other_recv = swap_x(other_keys)

    near = ready(push_weight, own, above, below, numerator, first_moment, second_moment)
    message, sent, first_new, second_new = step(push_weight, *near, up, down)
    bit_count = lax.axis_size("rep").bit_length() - 1
    branches = [partial(push_by, 1 << exponent) for exponent in range(bit_count)]
    message = lax.optimization_barrier((message, other_keys))[0]
    received = lax.switch(gossip_step[0] % bit_count, branches, message)
    numerator_new, weight_new = mix(push_weight, sent, received)
    other_recv = lax.optimization_barrier((other_recv, received))[0]
    keys = finish_keys(own_keys, other_recv, cosine, sine)
    return (keys, numerator_new, first_new, second_new, weight_new[0, :1])


def solution(mesh):
    in_specs = (
        P(("rep", "fsdp"), None),
        P("rep", None),
        P("rep", "fsdp"),
        P(("rep", "fsdp"), None),
        P("rep", "fsdp", None),
        P("rep", "fsdp", None),
        P("rep", "fsdp", None),
        P("rep"),
        P(),
    )
    out_specs = (
        P(("rep", "fsdp"), None),
        P("rep", "fsdp", None),
        P("rep", "fsdp", None),
        P("rep", "fsdp", None),
        P("rep"),
    )
    return jax.shard_map(local, mesh=mesh, in_specs=in_specs, out_specs=out_specs, check_vma=False)
```

```python
from functools import partial

import jax
import jax.numpy as jnp
from jax import lax
from jax.experimental import pallas as pl
from jax.experimental.pallas import tpu as pltpu
from jax.sharding import PartitionSpec as P

D = 4096
KVH = 4
HD = 128
DOCS = 8
KW = 512
TOK = 192
NZ = 8
ROWS = 256
STEP = 48
CHUNKS = TOK // STEP
HALF = NZ * ROWS
FIRST = (3, 1, 5, 7, 4)
REST = (2, 6, 0)


THETA = 1000000.0
BETA_ONE = 0.9
BETA_TWO = 0.95
STEP_RATE = 0.1
WEIGHT_DECAY = 0.2
EPSILON = 1e-08
NORM_EPSILON = 1e-05
FIRST_CORRECTION = 1.0 - 0.9**10
SECOND_CORRECTION = 1.0 - 0.95**10
SCALE = D ** (-0.5)

PARAMS = pltpu.CompilerParams(vmem_limit_bytes=16 * 1024 * 1024)
LARGE = pltpu.CompilerParams(vmem_limit_bytes=57 * 1024 * 1024)
F32, BF16 = jnp.float32, jnp.bfloat16


def along_z(value, distance):
    route = [(f, ((f // 2 + distance) % NZ) * 2 + f % 2) for f in range(2 * NZ)]
    return lax.ppermute(value, "fsdp", route)


def along_z_by_core(value, distance):
    route = []
    for r in range(lax.axis_size("rep")):
        way = distance if r % 2 == 0 else -distance
        for f in range(2 * NZ):
            route.append((r * 2 * NZ + f, r * 2 * NZ + ((f // 2 + way) % NZ) * 2 + f % 2))
    return lax.ppermute(value, ("rep", "fsdp"), route)


def swap_x(value):
    return lax.ppermute(value, "fsdp", [(f, f ^ 1) for f in range(2 * NZ)])


def whole(n):
    return [pl.BlockSpec(memory_space=pltpu.VMEM)] * n


def shapes(*pairs):
    return tuple(jax.ShapeDtypeStruct(shape, dtype) for shape, dtype in pairs)


def cost(size):
    return pl.CostEstimate(flops=0, bytes_accessed=size, transcendentals=0)


def place_of(z, o, side):
    return pl.ds(pl.multiple_of((2 * lax.rem(z + o, NZ) + side) * ROWS, ROWS), ROWS)


def place():
    f = lax.axis_index("fsdp")
    return lax.div(f, 2), lax.rem(f, 2)


def even_core():
    return lax.rem(lax.axis_index("rep"), 2) == 0


def scale_kernel(
    weight, tokens, gain, cotangent, numerator, send_first, scales, model, held, gains, shard, sems
):
    z, x = place()
    copies = [pltpu.make_async_copy(gain, gains, sems.at[0])]
    for n in range(CHUNKS):
        rows = pl.ds(n * STEP, STEP)
        copies.append(pltpu.make_async_copy(tokens.at[rows], held.at[rows], sems.at[n + 1]))
    columns = pl.ds(len(FIRST) * ROWS, KW)
    copies.append(pltpu.make_async_copy(cotangent, send_first.at[:, columns], sems.at[CHUNKS + 1]))
    copies.append(pltpu.make_async_copy(numerator.at[0], shard, sems.at[CHUNKS + 2]))
    for copy in copies:
        copy.start()
    copies[0].wait()

    def rows_of(i, carry):
        rows = pl.ds(pl.multiple_of(i * 16, 16), 16)
        values = held[rows, :].astype(F32)
        scale = lax.rsqrt(jnp.mean(values * values, axis=-1, keepdims=True) + NORM_EPSILON)
        scales[rows, :] = jnp.broadcast_to(scale, (16, 128))
        for n, o in enumerate(FIRST):
            columns = place_of(z, o, 1 - x)
            part = held[rows, columns].astype(F32) * scale * gains[:, columns]
            send_first[rows, n * ROWS : (n + 1) * ROWS] = part.astype(BF16)
        return carry

    for n in range(CHUNKS):
        copies[n + 1].wait()
        lax.fori_loop(n * STEP // 16, (n + 1) * STEP // 16, rows_of, 0)
    copies[-2].wait()
    copies[-1].wait()
    model[...] = (shard[...] / weight[0]).astype(BF16)


def normalise_first(weight, *operands):
    return pl.pallas_call(
        scale_kernel,
        out_shape=shapes(
            ((TOK, len(FIRST) * ROWS + KW), BF16),
            ((TOK, 128), F32),
            ((ROWS, KW), BF16),
        ),
        in_specs=[pl.BlockSpec(memory_space=pltpu.SMEM)] + [pl.BlockSpec(memory_space=pltpu.HBM)] * 4,
        out_specs=whole(3),
        scratch_shapes=[
            pltpu.VMEM((TOK, D), BF16),
            pltpu.VMEM((1, D), F32),
            pltpu.VMEM((ROWS, KW), F32),
            pltpu.SemaphoreType.DMA((CHUNKS + 3,)),
        ],
        compiler_params=LARGE,
        cost_estimate=cost(1 << 10),
        name="normalise_first",
    )(weight, *operands)


def norm_kernel(tokens, gain, scales, keep, send_rest):
    z, x = place()

    def rows_of(i, carry):
        rows = pl.ds(pl.multiple_of(i * 16, 16), 16)
        scale = scales[rows, :1]

        def part(o, side):
            columns = place_of(z, o, side)
            return (tokens[rows, columns].astype(F32) * scale * gain[:, columns]).astype(BF16)

        for n, o in enumerate(FIRST + REST):
            keep[rows, n * ROWS : (n + 1) * ROWS] = part(o, x)
        for n, o in enumerate(REST):
            send_rest[rows, n * ROWS : (n + 1) * ROWS] = part(o, 1 - x)
        return carry

    lax.fori_loop(0, TOK // 16, rows_of, 0)


def normalise(*operands):
    return pl.pallas_call(
        norm_kernel,
        out_shape=shapes(((TOK, HALF), BF16), ((TOK, len(REST) * ROWS), BF16)),
        in_specs=whole(3),
        out_specs=whole(2),
        compiler_params=PARAMS,
        cost_estimate=cost(1 << 10),
        name="normalise",
    )(*operands)


def rotate_rows(cotangent, cosine, sine):
    parts = []
    for h in range(KVH):
        y = cotangent[:, h * HD : (h + 1) * HD].astype(F32)
        s = y * sine
        turned = jnp.concatenate([-s[:, HD // 2 :], s[:, : HD // 2]], axis=-1)
        parts.append(((y * cosine - turned) * SCALE).astype(BF16))
    return jnp.concatenate(parts, axis=-1)


OVER = (((0,), (0,)), ((), ()))


def grad_block(keep, recv, back, n):
    return lax.dot_general(
        keep[:, n * ROWS : (n + 1) * ROWS], back[:TOK], OVER, preferred_element_type=F32
    ) + lax.dot_general(recv[:, n * ROWS : (n + 1) * ROWS], back[TOK:], OVER, preferred_element_type=F32)


def first_kernel(keep, recv, cotangent, cosine, sine, up, down, four, back):
    back[:TOK] = rotate_rows(cotangent[...], cosine[:TOK], sine[:TOK])
    back[TOK:] = rotate_rows(recv[:, len(FIRST) * ROWS :], cosine[TOK:], sine[TOK:])
    for n, target in enumerate((up.at[:ROWS], up.at[ROWS:], down.at[:ROWS], down.at[ROWS:], four)):
        target[...] = grad_block(keep, recv, back, n).astype(BF16)


def first_parts(keep, recv, cotangent, cosine, sine):
    return pl.pallas_call(
        first_kernel,
        out_shape=shapes(*[((2 * ROWS, KW), BF16)] * 2, ((ROWS, KW), BF16), ((2 * TOK, KW), BF16)),
        in_specs=whole(5),
        out_specs=whole(4),
        compiler_params=PARAMS,
        cost_estimate=cost(1 << 10),
        name="first_parts",
    )(keep, recv, cotangent, cosine, sine)


def rest_parts(keep, recv, back):
    columns = keep[:, len(FIRST) * ROWS :]
    return lax.dot_general(columns, back[:TOK], OVER, preferred_element_type=F32) + lax.dot_general(
        recv, back[TOK:], OVER, preferred_element_type=F32
    )


def turn_kernel(own, above, below, four, up, down, near):
    near[...] = own[2 * ROWS :] + above[ROWS:].astype(F32) + below[ROWS:].astype(F32)
    extra = four[...].astype(F32)
    share = jnp.full((ROWS, KW), even_core().astype(F32)) > 0.5
    up[...] = (own[:ROWS] + above[:ROWS].astype(F32) + jnp.where(share, extra, 0.0)).astype(BF16)
    down[...] = (own[ROWS : 2 * ROWS] + below[:ROWS].astype(F32) + jnp.where(share, 0.0, extra)).astype(BF16)


def turn(*operands):
    return pl.pallas_call(
        turn_kernel,
        out_shape=shapes(*[((ROWS, KW), BF16)] * 2, ((ROWS, KW), F32)),
        in_specs=whole(4),
        out_specs=whole(3),
        compiler_params=PARAMS,
        cost_estimate=cost(1 << 10),
        name="turn",
    )(*operands)


def second_kernel(zero, two, six, above, below, far):
    for target, parts in ((above, (zero, six)), (below, (zero, two))):
        for n, part in enumerate(parts):
            target[n * ROWS : (n + 1) * ROWS] = part[...]
    share = jnp.full((ROWS, KW), even_core().astype(F32)) > 0.5
    far[...] = jnp.where(share, six[...].astype(F32), two[...].astype(F32)).astype(BF16)


def second_rows(*operands):
    return pl.pallas_call(
        second_kernel,
        out_shape=shapes(*[((2 * ROWS, KW), BF16)] * 2, ((ROWS, KW), BF16)),
        in_specs=whole(3),
        out_specs=whole(3),
        compiler_params=PARAMS,
        cost_estimate=cost(1 << 10),
        name="second_rows",
    )(*operands)


def keys_kernel(keep, first, rest, zero, two, six, below, above, far, own, other):
    model = {0: zero[...], 2: two[...], 6: six[...], 4: far[...]}
    model.update({1: below[:ROWS], 3: below[ROWS:], 7: above[:ROWS], 5: above[ROWS:]})
    total = jnp.zeros((TOK, KW), F32)
    for blocks, ref in ((FIRST, first), (REST, rest)):
        for n, o in enumerate(blocks):
            total += jnp.dot(ref[:, n * ROWS : (n + 1) * ROWS], model[o], preferred_element_type=F32)
    other[...] = total.astype(BF16)
    total = jnp.zeros((TOK, KW), F32)
    for n, o in enumerate(FIRST + REST):
        total += jnp.dot(keep[:, n * ROWS : (n + 1) * ROWS], model[o], preferred_element_type=F32)
    own[...] = total


def keys_parts(*operands):
    return pl.pallas_call(
        keys_kernel,
        out_shape=shapes(((TOK, KW), F32), ((TOK, KW), BF16)),
        in_specs=whole(9),
        out_specs=whole(2),
        compiler_params=PARAMS,
        cost_estimate=cost(1 << 10),
        name="keys_parts",
    )(*operands)


def ready_kernel(weight, numerator, first, second, shard, moment, square):
    shard[...] = numerator[0] * (0.5 - 0.5 * STEP_RATE * WEIGHT_DECAY / weight[0])
    moment[...] = BETA_ONE * first[0]
    square[...] = BETA_TWO * second[0]


def ready(weight, *operands):
    return pl.pallas_call(
        ready_kernel,
        out_shape=shapes(*[((ROWS, KW), F32)] * 3),
        in_specs=[pl.BlockSpec(memory_space=pltpu.SMEM)] + whole(3),
        out_specs=whole(3),
        compiler_params=PARAMS,
        cost_estimate=cost(1 << 10),
        name="ready",
    )(weight, *operands)


def step(push_weight, near, shard, moment, square, up, down):
    grad = near + up.astype(F32) + down.astype(F32)
    first = moment + (1.0 - BETA_ONE) * grad
    second = square + (1.0 - BETA_TWO) * grad * grad
    root = jnp.sqrt(second * (1.0 / SECOND_CORRECTION)) + EPSILON
    half = shard - first * (0.5 * STEP_RATE / FIRST_CORRECTION) / root
    message = jnp.concatenate([half, jnp.broadcast_to(0.5 * push_weight[:, None], (16, KW))]).astype(BF16)
    return message, half, first[None], second[None]


def last_kernel(weight, sent, received, own, other, cosine, sine, keys, numerator_new, weight_new):
    numerator_new[0] = sent[...] + received[:ROWS].astype(F32)
    weight_new[...] = 0.5 * weight[0] + received[ROWS : ROWS + 1, :128].astype(F32)
    for h in range(KVH):
        columns = slice(h * HD, (h + 1) * HD)
        pre = (own[:, columns] + other[:, columns].astype(F32)) * SCALE
        turned = jnp.concatenate([-pre[:, HD // 2 :], pre[:, : HD // 2]], axis=-1)
        keys[:, columns] = (pre * cosine[:TOK] + turned * sine[:TOK]).astype(BF16)


def last(weight, *operands):
    return pl.pallas_call(
        last_kernel,
        out_shape=shapes(((TOK, KW), BF16), ((1, ROWS, KW), F32), ((1, 128), F32)),
        in_specs=[pl.BlockSpec(memory_space=pltpu.SMEM)] + whole(6),
        out_specs=whole(3),
        compiler_params=PARAMS,
        cost_estimate=cost(1 << 10),
        name="last",
    )(weight, *operands)


def push_by(distance, message):
    n = lax.axis_size("rep")
    return lax.ppermute(message, "rep", [((i - distance) % n, i) for i in range(n)])


def local(
    tokens,
    norm_gain,
    doc_ids,
    key_cotangent,
    numerator,
    first_moment,
    second_moment,
    push_weight,
    gossip_step,
):
    f = lax.axis_index("fsdp")
    x = f % 2


    send_first, scales, model = normalise_first(push_weight, tokens, norm_gain, key_cotangent, numerator)
    recv_first = swap_x(send_first)
    ids = jnp.broadcast_to(doc_ids[None], (2 * NZ, 1, TOK))
    ids = lax.all_to_all(ids, "fsdp", 0, 0, tiled=True)
    scales, ids, model = lax.optimization_barrier((scales, ids, model))
    keep, send_rest = normalise(tokens, norm_gain, scales)
    documents = jnp.arange(DOCS, dtype=jnp.int32)
    totals = jnp.sum((ids.reshape(1, -1) == documents[:, None]).astype(jnp.int32), axis=1)
    other = f + 1 - 2 * x
    pair_ids = jnp.concatenate([doc_ids[0], lax.dynamic_index_in_dim(ids, other, 0, False)[0]])
    row = jnp.arange(TOK, dtype=jnp.int32)
    index = jnp.concatenate([f * TOK + row, other * TOK + row])
    starts = jnp.sum(jnp.where(pair_ids[:, None] > documents[None, :], totals[None, :], 0), axis=1)
    positions = index - starts
    frequency = THETA ** (-(jnp.arange(HD // 2, dtype=jnp.float32) * 2.0 / HD))
    frequency = jnp.concatenate([frequency, frequency])
    angles = positions.astype(jnp.float32)[:, None] * frequency[None, :]
    cosine, sine = jnp.cos(angles), jnp.sin(angles)

    above, below, four, back = first_parts(keep, recv_first, key_cotangent, cosine, sine)
    above, below, four = along_z(above, 1), along_z(below, -1), along_z_by_core(four, 2)
    recv_rest = swap_x(send_rest)
    six, two = along_z(model, 2), along_z(model, -2)
    own = rest_parts(keep, recv_rest, back)
    model, six, two, own = lax.optimization_barrier((model, six, two, own))
    rows_above, rows_below, far = second_rows(model, two, six)
    rows_above, rows_below = along_z(rows_above, 1), along_z(rows_below, -1)
    far = along_z_by_core(far, 2)

    up, down, near = turn(own, above, below, four)
    up, down = along_z(up, 2), along_z(down, -2)

    own_keys, other_keys = keys_parts(
        keep, recv_first, recv_rest, model, two, six, rows_below, rows_above, far
    )
    other_recv = swap_x(other_keys)

    gated = lax.optimization_barrier((numerator, other_keys))[0]
    parts = ready(push_weight, gated, first_moment, second_moment)
    message, sent, first_new, second_new = step(push_weight, near, *parts, up, down)
    bit_count = lax.axis_size("rep").bit_length() - 1
    branches = [partial(push_by, 1 << exponent) for exponent in range(bit_count)]
    message = lax.optimization_barrier((message, other_keys))[0]
    received = lax.switch(gossip_step[0] % bit_count, branches, message)
    other_recv = lax.optimization_barrier((other_recv, received))[0]
    keys, numerator_new, weight_new = last(push_weight, sent, received, own_keys, other_recv, cosine, sine)
    return (keys, numerator_new, first_new, second_new, weight_new[0, :1])


def solution(mesh):
    in_specs = (
        P(("rep", "fsdp"), None),
        P("rep", None),
        P("rep", "fsdp"),
        P(("rep", "fsdp"), None),
        P("rep", "fsdp", None),
        P("rep", "fsdp", None),
        P("rep", "fsdp", None),
        P("rep"),
        P(),
    )
    out_specs = (
        P(("rep", "fsdp"), None),
        P("rep", "fsdp", None),
        P("rep", "fsdp", None),
        P("rep", "fsdp", None),
        P("rep"),
    )
    return jax.shard_map(local, mesh=mesh, in_specs=in_specs, out_specs=out_specs, check_vma=False)
```

```python
from functools import partial

import jax
import jax.numpy as jnp
from jax import lax
from jax.experimental import pallas as pl
from jax.experimental.pallas import tpu as pltpu
from jax.sharding import PartitionSpec as P

D = 4096
KVH = 4
HD = 128
DOCS = 8
KW = 512
TOK = 192
NZ = 8
ROWS = 256
STEP = 48
CHUNKS = TOK // STEP
HALF = NZ * ROWS
FIRST = (3, 1, 5, 7, 4)
REST = (2, 6, 0)


THETA = 1000000.0
BETA_ONE = 0.9
BETA_TWO = 0.95
STEP_RATE = 0.1
WEIGHT_DECAY = 0.2
EPSILON = 1e-08
NORM_EPSILON = 1e-05
FIRST_CORRECTION = 1.0 - 0.9**10
SECOND_CORRECTION = 1.0 - 0.95**10
SCALE = D ** (-0.5)

PARAMS = pltpu.CompilerParams(vmem_limit_bytes=16 * 1024 * 1024)
LARGE = pltpu.CompilerParams(vmem_limit_bytes=57 * 1024 * 1024)
F32, BF16 = jnp.float32, jnp.bfloat16


def along_z(value, distance):
    route = [(f, ((f // 2 + distance) % NZ) * 2 + f % 2) for f in range(2 * NZ)]
    return lax.ppermute(value, "fsdp", route)


def along_z_by_core(value, distance):
    route = []
    for r in range(lax.axis_size("rep")):
        way = distance if r % 2 == 0 else -distance
        for f in range(2 * NZ):
            route.append((r * 2 * NZ + f, r * 2 * NZ + ((f // 2 + way) % NZ) * 2 + f % 2))
    return lax.ppermute(value, ("rep", "fsdp"), route)


def swap_x(value):
    return lax.ppermute(value, "fsdp", [(f, f ^ 1) for f in range(2 * NZ)])


def whole(n):
    return [pl.BlockSpec(memory_space=pltpu.VMEM)] * n


def shapes(*pairs):
    return tuple(jax.ShapeDtypeStruct(shape, dtype) for shape, dtype in pairs)


def cost(size):
    return pl.CostEstimate(flops=0, bytes_accessed=size, transcendentals=0)


def place_of(z, o, side):
    return pl.ds(pl.multiple_of((2 * lax.rem(z + o, NZ) + side) * ROWS, ROWS), ROWS)


def place():
    f = lax.axis_index("fsdp")
    return lax.div(f, 2), lax.rem(f, 2)


def even_core():
    return lax.rem(lax.axis_index("rep"), 2) == 0


def scale_kernel(
    weight, tokens, gain, cotangent, numerator, send_first, scales, model, held, gains, shard, sems
):
    z, x = place()
    copies = [pltpu.make_async_copy(gain, gains, sems.at[0])]
    for n in range(CHUNKS):
        rows = pl.ds(n * STEP, STEP)
        copies.append(pltpu.make_async_copy(tokens.at[rows], held.at[rows], sems.at[n + 1]))
    columns = pl.ds(len(FIRST) * ROWS, KW)
    copies.append(pltpu.make_async_copy(cotangent, send_first.at[:, columns], sems.at[CHUNKS + 1]))
    copies.append(pltpu.make_async_copy(numerator.at[0], shard, sems.at[CHUNKS + 2]))
    for copy in copies:
        copy.start()
    copies[0].wait()

    def rows_of(i, carry):
        rows = pl.ds(pl.multiple_of(i * 16, 16), 16)
        values = held[rows, :].astype(F32)
        scale = lax.rsqrt(jnp.mean(values * values, axis=-1, keepdims=True) + NORM_EPSILON)
        scales[rows, :] = jnp.broadcast_to(scale, (16, 128))
        for n, o in enumerate(FIRST):
            columns = place_of(z, o, 1 - x)
            part = held[rows, columns].astype(F32) * scale * gains[:, columns]
            send_first[rows, n * ROWS : (n + 1) * ROWS] = part.astype(BF16)
        return carry

    for n in range(CHUNKS):
        copies[n + 1].wait()
        lax.fori_loop(n * STEP // 16, (n + 1) * STEP // 16, rows_of, 0)
    copies[-2].wait()
    copies[-1].wait()
    model[...] = (shard[...] / weight[0]).astype(BF16)


def normalise_first(weight, *operands):
    return pl.pallas_call(
        scale_kernel,
        out_shape=shapes(
            ((TOK, len(FIRST) * ROWS + KW), BF16),
            ((TOK, 128), F32),
            ((ROWS, KW), BF16),
        ),
        in_specs=[pl.BlockSpec(memory_space=pltpu.SMEM)] + [pl.BlockSpec(memory_space=pltpu.HBM)] * 4,
        out_specs=whole(3),
        scratch_shapes=[
            pltpu.VMEM((TOK, D), BF16),
            pltpu.VMEM((1, D), F32),
            pltpu.VMEM((ROWS, KW), F32),
            pltpu.SemaphoreType.DMA((CHUNKS + 3,)),
        ],
        compiler_params=LARGE,
        cost_estimate=cost(1 << 10),
        name="normalise_first",
    )(weight, *operands)


def norm_kernel(tokens, gain, scales, keep, send_rest):
    z, x = place()

    def rows_of(i, carry):
        rows = pl.ds(pl.multiple_of(i * 16, 16), 16)
        scale = scales[rows, :1]

        def part(o, side):
            columns = place_of(z, o, side)
            return (tokens[rows, columns].astype(F32) * scale * gain[:, columns]).astype(BF16)

        for n, o in enumerate(FIRST + REST):
            keep[rows, n * ROWS : (n + 1) * ROWS] = part(o, x)
        for n, o in enumerate(REST):
            send_rest[rows, n * ROWS : (n + 1) * ROWS] = part(o, 1 - x)
        return carry

    lax.fori_loop(0, TOK // 16, rows_of, 0)


def normalise(*operands):
    return pl.pallas_call(
        norm_kernel,
        out_shape=shapes(((TOK, HALF), BF16), ((TOK, len(REST) * ROWS), BF16)),
        in_specs=whole(3),
        out_specs=whole(2),
        compiler_params=PARAMS,
        cost_estimate=cost(1 << 10),
        name="normalise",
    )(*operands)


def rotate_rows(cotangent, cosine, sine):
    parts = []
    for h in range(KVH):
        y = cotangent[:, h * HD : (h + 1) * HD].astype(F32)
        s = y * sine
        turned = jnp.concatenate([-s[:, HD // 2 :], s[:, : HD // 2]], axis=-1)
        parts.append(((y * cosine - turned) * SCALE).astype(BF16))
    return jnp.concatenate(parts, axis=-1)


OVER = (((0,), (0,)), ((), ()))


def grad_block(keep, recv, back, n):
    return lax.dot_general(
        keep[:, n * ROWS : (n + 1) * ROWS], back[:TOK], OVER, preferred_element_type=F32
    ) + lax.dot_general(recv[:, n * ROWS : (n + 1) * ROWS], back[TOK:], OVER, preferred_element_type=F32)


def first_kernel(keep, recv, cotangent, cosine, sine, up, down, four, back):
    back[:TOK] = rotate_rows(cotangent[...], cosine[:TOK], sine[:TOK])
    back[TOK:] = rotate_rows(recv[:, len(FIRST) * ROWS :], cosine[TOK:], sine[TOK:])
    for n, target in enumerate((up.at[:ROWS], up.at[ROWS:], down.at[:ROWS], down.at[ROWS:], four)):
        target[...] = grad_block(keep, recv, back, n).astype(BF16)


def first_parts(keep, recv, cotangent, cosine, sine):
    return pl.pallas_call(
        first_kernel,
        out_shape=shapes(*[((2 * ROWS, KW), BF16)] * 2, ((ROWS, KW), BF16), ((2 * TOK, KW), BF16)),
        in_specs=whole(5),
        out_specs=whole(4),
        compiler_params=PARAMS,
        cost_estimate=cost(1 << 10),
        name="first_parts",
    )(keep, recv, cotangent, cosine, sine)


def rest_parts(keep, recv, back):
    columns = keep[:, len(FIRST) * ROWS :]
    return lax.dot_general(columns, back[:TOK], OVER, preferred_element_type=F32) + lax.dot_general(
        recv, back[TOK:], OVER, preferred_element_type=F32
    )


def turn_kernel(own, above, below, four, up, down, near):
    near[...] = own[2 * ROWS :] + above[ROWS:].astype(F32) + below[ROWS:].astype(F32)
    extra = four[...].astype(F32)
    share = jnp.full((ROWS, KW), even_core().astype(F32)) > 0.5
    up[...] = (own[:ROWS] + above[:ROWS].astype(F32) + jnp.where(share, extra, 0.0)).astype(BF16)
    down[...] = (own[ROWS : 2 * ROWS] + below[:ROWS].astype(F32) + jnp.where(share, 0.0, extra)).astype(BF16)


def turn(*operands):
    return pl.pallas_call(
        turn_kernel,
        out_shape=shapes(*[((ROWS, KW), BF16)] * 2, ((ROWS, KW), F32)),
        in_specs=whole(4),
        out_specs=whole(3),
        compiler_params=PARAMS,
        cost_estimate=cost(1 << 10),
        name="turn",
    )(*operands)


def second_kernel(zero, two, six, above, below, far):
    for target, parts in ((above, (zero, six)), (below, (zero, two))):
        for n, part in enumerate(parts):
            target[n * ROWS : (n + 1) * ROWS] = part[...]
    share = jnp.full((ROWS, KW), even_core().astype(F32)) > 0.5
    far[...] = jnp.where(share, six[...].astype(F32), two[...].astype(F32)).astype(BF16)


def second_rows(*operands):
    return pl.pallas_call(
        second_kernel,
        out_shape=shapes(*[((2 * ROWS, KW), BF16)] * 2, ((ROWS, KW), BF16)),
        in_specs=whole(3),
        out_specs=whole(3),
        compiler_params=PARAMS,
        cost_estimate=cost(1 << 10),
        name="second_rows",
    )(*operands)


def keys_kernel(keep, first, rest, zero, two, six, below, above, far, own, other):
    model = {0: zero[...], 2: two[...], 6: six[...], 4: far[...]}
    model.update({1: below[:ROWS], 3: below[ROWS:], 7: above[:ROWS], 5: above[ROWS:]})
    total = jnp.zeros((TOK, KW), F32)
    for blocks, ref in ((FIRST, first), (REST, rest)):
        for n, o in enumerate(blocks):
            total += jnp.dot(ref[:, n * ROWS : (n + 1) * ROWS], model[o], preferred_element_type=F32)
    other[...] = total.astype(BF16)
    total = jnp.zeros((TOK, KW), F32)
    for n, o in enumerate(FIRST + REST):
        total += jnp.dot(keep[:, n * ROWS : (n + 1) * ROWS], model[o], preferred_element_type=F32)
    own[...] = total


def keys_parts(*operands):
    return pl.pallas_call(
        keys_kernel,
        out_shape=shapes(((TOK, KW), F32), ((TOK, KW), BF16)),
        in_specs=whole(9),
        out_specs=whole(2),
        compiler_params=PARAMS,
        cost_estimate=cost(1 << 10),
        name="keys_parts",
    )(*operands)


def ready_kernel(weight, numerator, first, second, shard, moment, square):
    shard[...] = numerator[0] * (0.5 - 0.5 * STEP_RATE * WEIGHT_DECAY / weight[0])
    moment[...] = BETA_ONE * first[0]
    square[...] = BETA_TWO * second[0]


def ready(weight, *operands):
    return pl.pallas_call(
        ready_kernel,
        out_shape=shapes(*[((ROWS, KW), F32)] * 3),
        in_specs=[pl.BlockSpec(memory_space=pltpu.SMEM)] + whole(3),
        out_specs=whole(3),
        compiler_params=PARAMS,
        cost_estimate=cost(1 << 10),
        name="ready",
    )(weight, *operands)


def step(push_weight, near, shard, moment, square, up, down):
    grad = near + up.astype(F32) + down.astype(F32)
    first = moment + (1.0 - BETA_ONE) * grad
    second = square + (1.0 - BETA_TWO) * grad * grad
    root = jnp.sqrt(second * (1.0 / SECOND_CORRECTION)) + EPSILON
    half = shard - first * (0.5 * STEP_RATE / FIRST_CORRECTION) / root
    message = jnp.concatenate([half, jnp.broadcast_to(0.5 * push_weight[:, None], (16, KW))]).astype(BF16)
    return message, half, first[None], second[None]


def last_kernel(weight, sent, received, own, other, cosine, sine, keys, numerator_new, weight_new):
    numerator_new[0] = sent[...] + received[:ROWS].astype(F32)
    weight_new[...] = 0.5 * weight[0] + received[ROWS : ROWS + 1, :128].astype(F32)
    for h in range(KVH):
        columns = slice(h * HD, (h + 1) * HD)
        pre = (own[:, columns] + other[:, columns].astype(F32)) * SCALE
        turned = jnp.concatenate([-pre[:, HD // 2 :], pre[:, : HD // 2]], axis=-1)
        keys[:, columns] = (pre * cosine[:TOK] + turned * sine[:TOK]).astype(BF16)


def last(weight, *operands):
    return pl.pallas_call(
        last_kernel,
        out_shape=shapes(((TOK, KW), BF16), ((1, ROWS, KW), F32), ((1, 128), F32)),
        in_specs=[pl.BlockSpec(memory_space=pltpu.SMEM)] + whole(6),
        out_specs=whole(3),
        compiler_params=PARAMS,
        cost_estimate=cost(1 << 10),
        name="last",
    )(weight, *operands)


def push_by(distance, message, other_keys):
    n = lax.axis_size("rep")
    received = lax.ppermute(message, "rep", [((i - distance) % n, i) for i in range(n)])
    return received, swap_x(other_keys)


def local(
    tokens,
    norm_gain,
    doc_ids,
    key_cotangent,
    numerator,
    first_moment,
    second_moment,
    push_weight,
    gossip_step,
):
    f = lax.axis_index("fsdp")
    x = f % 2


    send_first, scales, model = normalise_first(push_weight, tokens, norm_gain, key_cotangent, numerator)
    recv_first = swap_x(send_first)
    ids = jnp.broadcast_to(doc_ids[None], (2 * NZ, 1, TOK))
    ids = lax.all_to_all(ids, "fsdp", 0, 0, tiled=True)
    scales, ids, model = lax.optimization_barrier((scales, ids, model))
    keep, send_rest = normalise(tokens, norm_gain, scales)
    documents = jnp.arange(DOCS, dtype=jnp.int32)
    totals = jnp.sum((ids.reshape(1, -1) == documents[:, None]).astype(jnp.int32), axis=1)
    other = f + 1 - 2 * x
    pair_ids = jnp.concatenate([doc_ids[0], lax.dynamic_index_in_dim(ids, other, 0, False)[0]])
    row = jnp.arange(TOK, dtype=jnp.int32)
    index = jnp.concatenate([f * TOK + row, other * TOK + row])
    starts = jnp.sum(jnp.where(pair_ids[:, None] > documents[None, :], totals[None, :], 0), axis=1)
    positions = index - starts
    frequency = THETA ** (-(jnp.arange(HD // 2, dtype=jnp.float32) * 2.0 / HD))
    frequency = jnp.concatenate([frequency, frequency])
    angles = positions.astype(jnp.float32)[:, None] * frequency[None, :]
    cosine, sine = jnp.cos(angles), jnp.sin(angles)

    above, below, four, back = first_parts(keep, recv_first, key_cotangent, cosine, sine)
    above, below, four = along_z(above, 1), along_z(below, -1), along_z_by_core(four, 2)
    recv_rest = swap_x(send_rest)
    six, two = along_z(model, 2), along_z(model, -2)
    own = rest_parts(keep, recv_rest, back)
    model, six, two, own = lax.optimization_barrier((model, six, two, own))
    rows_above, rows_below, far = second_rows(model, two, six)
    rows_above, rows_below = along_z(rows_above, 1), along_z(rows_below, -1)
    far = along_z_by_core(far, 2)

    up, down, near = turn(own, above, below, four)
    up, down = along_z(up, 2), along_z(down, -2)

    own_keys, other_keys = keys_parts(
        keep, recv_first, recv_rest, model, two, six, rows_below, rows_above, far
    )

    gated = lax.optimization_barrier((numerator, other_keys))[0]
    parts = ready(push_weight, gated, first_moment, second_moment)
    message, sent, first_new, second_new = step(push_weight, near, *parts, up, down)
    bit_count = lax.axis_size("rep").bit_length() - 1
    branches = [partial(push_by, 1 << exponent) for exponent in range(bit_count)]
    received, other_recv = lax.switch(gossip_step[0] % bit_count, branches, message, other_keys)
    keys, numerator_new, weight_new = last(push_weight, sent, received, own_keys, other_recv, cosine, sine)
    return (keys, numerator_new, first_new, second_new, weight_new[0, :1])


def solution(mesh):
    in_specs = (
        P(("rep", "fsdp"), None),
        P("rep", None),
        P("rep", "fsdp"),
        P(("rep", "fsdp"), None),
        P("rep", "fsdp", None),
        P("rep", "fsdp", None),
        P("rep", "fsdp", None),
        P("rep"),
        P(),
    )
    out_specs = (
        P(("rep", "fsdp"), None),
        P("rep", "fsdp", None),
        P("rep", "fsdp", None),
        P("rep", "fsdp", None),
        P("rep"),
    )
    return jax.shard_map(local, mesh=mesh, in_specs=in_specs, out_specs=out_specs, check_vma=False)
```
